32 devices in a mesh: seq: 16 (over z, y, core), tp: 2 (over x).
Axes of the slice: x: 2, y: 2, z: 4, core: 2. Of those that a mesh axis runs over, the one named last changes fastest.
Arguments:
- cache: bfloat16 [2, 16, 512, 3072], P(None, 'seq', 'tp'), may hold values from -24 to 24
- cache_len: int32 [16], replicated, may hold values from 1 to 512, 4096 in all
- group: bfloat16 [3, 16, 256, 3072], P(None, 'seq', None, 'tp'), may hold values from -24 to 24
- group_req: int32 [16], replicated, may hold values from 0 to 15, each once
- req_order: int32 [16], replicated, may hold values from 0 to 15, each once
Outputs:
- context: bfloat16 [16, 256, 3072], P('seq', None, 'tp')
The draws below stay inside these ranges and needn't reach their ends.
Inputs may be any that keep to these rules, and one draw needn't show every extreme that they name: `group_req`: each request once. `req_order`: each request once.
All inputs are finite; a program needn't handle non-finite values.
Results may differ from the reference program's by a relative error of at most 0.0042.
Values may be sent and summed in bfloat16 or wider, within the bound.
A program may use at most 64 MiB of HBM per device.

```python
import math
import jax
import jax.numpy as jnp
import numpy as np
from jax import lax

HEADS = 32
HD = 96
MAXLEN = 512
GROUP = 256
REQS = 16


def draw_cache(key, part):
    local_key = jax.random.fold_in(key, 1)
    array_dims = (2, REQS, MAXLEN, HEADS * HD)
    entries = jnp.clip(jax.random.normal(local_key, array_dims, jnp.float32), -4.0, 4.0)
    return entries.astype(jnp.bfloat16)


def draw_group(key, part):
    local_key = jax.random.fold_in(key, 2)
    array_dims = (3, REQS, GROUP, HEADS * HD)
    entries = jnp.clip(jax.random.normal(local_key, array_dims, jnp.float32), -4.0, 4.0)
    return entries.astype(jnp.bfloat16)


def split_up(number_of, total, reach, lean):
    weights = [(1 << 20) // math.isqrt(rank ** lean) + 1 for rank in range(2, number_of + 1)]
    spare, counts = total - reach - (number_of - 1), [1] * (number_of - 1)
    while spare > 0:
        candidates = [i for i in range(number_of - 1) if counts[i] < reach]
        whole, left = sum([weights[i] for i in candidates]), spare
        for i in candidates:
            more = min(reach - counts[i], max(1, left * weights[i] // whole), spare)
            counts[i] = counts[i] + more
            spare = spare - more
    return np.array([reach] + counts)


def uneven(key, number_of, total, most, skew):
    if number_of == 2:
        one = jax.random.randint(key, (), max(1, total - most), min(most, total - 1) + 1)
        return jnp.stack([one, total - one])
    sizes = jnp.asarray(split_up(number_of, total, most, skew), jnp.int32)
    twos = (number_of - 1) // 2
    source_of, receiver = sizes[1:1 + 2 * twos:2], sizes[2:2 + 2 * twos:2]
    slack = jnp.minimum(source_of - 1, most - receiver)
    shifted = jax.random.randint(jax.random.fold_in(key, 1), (twos,), 0, 1 << 20) % (slack + 1)
    sizes = sizes.at[1:1 + 2 * twos:2].set(source_of - shifted).at[2:2 + 2 * twos:2].set(receiver + shifted)
    return sizes[jax.random.permutation(jax.random.fold_in(key, 2), number_of)]


def setup_inputs(seed: int = 0) -> dict:
    splits = jax.random.split(jax.random.key(seed), 6)
    cache = draw_cache(jax.random.fold_in(splits[5], 71), 0)
    cache_len = uneven(splits[1], REQS, REQS * MAXLEN // 2, MAXLEN, 2).astype(jnp.int32)
    group = draw_group(jax.random.fold_in(splits[5], 71), 0)
    group_req = jax.random.permutation(splits[3], REQS).astype(jnp.int32)
    req_order = jax.random.permutation(splits[4], REQS).astype(jnp.int32)
    return {"cache": cache, "cache_len": cache_len, "group": group, "group_req": group_req, "req_order": req_order}


def inverse_table(permutation):
    numbers = jnp.arange(permutation.shape[0], dtype=jnp.int32)
    return jnp.zeros_like(numbers).at[permutation].set(numbers)

def partial_softmax(queries, key_rows, value_rows, allowed, factor):
    scores = jnp.einsum('qhd,khd->hqk', queries.astype(jnp.float32), key_rows.astype(jnp.float32)) * factor
    scores = jnp.where(allowed[None], scores, -jnp.inf)
    row_top = lax.optimization_barrier(jnp.max(scores, axis=-1))
    weights = jnp.exp(scores - row_top[..., None]).astype(jnp.bfloat16)
    weight_sum = lax.optimization_barrier(jnp.sum(weights.astype(jnp.float32), axis=-1))
    weighted = jnp.einsum('hqk,khd->hqd', weights.astype(jnp.float32), value_rows.astype(jnp.float32))
    return (row_top, weight_sum, weighted)

def combine_parts(first_part, second_part):
    top_one, sum_one, mixed_one = first_part
    top_two, sum_two, mixed_two = second_part
    row_top = jnp.maximum(top_one, top_two)
    factor_one = jnp.exp(top_one - row_top)
    factor_two = jnp.exp(top_two - row_top)
    result = (factor_one[..., None] * mixed_one + factor_two[..., None] * mixed_two) / (factor_one * sum_one + factor_two * sum_two)[..., None]
    result = jnp.transpose(result, (1, 0, 2))
    return result.reshape(result.shape[0], -1).astype(jnp.bfloat16)

def reference(cache, cache_len, group, group_req, req_order):
    factor = 1.0 / math.sqrt(HD)
    slot_of = inverse_table(req_order)
    causal = jnp.arange(GROUP)[:, None] >= jnp.arange(GROUP)[None, :]

    def one_device(device):
        request = group_req[device]
        cache_slot = slot_of[request]
        length = cache_len[request]
        queries = group[0, device].reshape(GROUP, HEADS, HD)
        new_keys = group[1, device].reshape(GROUP, HEADS, HD)
        new_values = group[2, device].reshape(GROUP, HEADS, HD)
        old_keys = cache[0, cache_slot].reshape(MAXLEN, HEADS, HD)
        old_values = cache[1, cache_slot].reshape(MAXLEN, HEADS, HD)
        allowed = (jnp.arange(MAXLEN) < length)[None, :]
        cache_part = partial_softmax(queries, old_keys, old_values, allowed, factor)
        group_part = partial_softmax(queries, new_keys, new_values, causal, factor)
        return combine_parts(cache_part, group_part)
    return lax.map(one_device, jnp.arange(REQS, dtype=jnp.int32))
```

```python
import functools
import math

import jax
import jax.numpy as jnp
from jax import lax
from jax.experimental import pallas as pl
from jax.experimental.pallas import tpu as pltpu
from jax.sharding import PartitionSpec as P

HD = 96
QUAD = 4 * HD
LANES = 128
MESH = pl.DeviceIdType.MESH
FACTOR = 1.0 / math.sqrt(HD)
WINDOWS = ((0, 128, 0), (0, 256, 96), (128, 256, 64), (256, 128, 32))


def attend(queries, key_rows, value_rows, keep, first_lane):
    width = queries.shape[1]
    lane = lax.broadcasted_iota(jnp.int32, (1, width), 1)
    mine = jnp.where((lane >= first_lane) & (lane < first_lane + HD), 1.0, 0.0)
    mask = mine.astype(jnp.bfloat16)
    rest = (1.0 - mine).astype(jnp.bfloat16)
    scores = lax.dot_general(
        queries * mask, key_rows, (((1,), (1,)), ((), ())), preferred_element_type=jnp.float32
    )
    scores = jnp.where(keep, scores, -jnp.inf)
    top = jnp.max(scores, axis=1, keepdims=True)
    weights = jnp.exp((scores - top) * FACTOR).astype(jnp.bfloat16)
    mixed = jnp.dot(weights, value_rows * mask + rest, preferred_element_type=jnp.float32)
    free = 0 if first_lane > 0 else HD
    total = mixed[:, free : free + 1]
    return mixed * (1.0 / total), top * FACTOR + jnp.log(total)


def attend_quad(load_queries, load_keys, load_values, keep):
    parts, logs = [], []
    for start, width, first_lane in WINDOWS:
        mix, log = attend(
            load_queries(start, width), load_keys(start, width), load_values(start, width), keep, first_lane
        )
        parts.append(mix)
        logs.append(log)
    lane = lax.broadcasted_iota(jnp.int32, (1, LANES), 1)
    tiles = (
        jnp.where(lane < 96, parts[0], parts[1][:, :LANES]),
        jnp.where(lane < 64, parts[1][:, LANES:], parts[2][:, :LANES]),
        jnp.where(lane < 32, parts[2][:, LANES:], parts[3]),
    )
    return tiles, logs


def kernel(
    n, tps, quads, source_ref, slot_ref, length_ref, cache_ref, group_ref, out_ref,
    kv, own, own_mix, own_log, old_log, *rest,
):
    spread, staged, asked, partial, landed, restaged, answer = (
        rest[i * quads : (i + 1) * quads] for i in range(7)
    )
    send_sem, recv_sem, kv_send, kv_recv, local_sem = rest[7 * quads :]
    me, tp = lax.axis_index("seq"), lax.axis_index("tp")
    rows = group_ref.shape[2]
    block = rows // n
    width = group_ref.shape[3]
    heads = width // HD
    positions = cache_ref.shape[2]
    my_rows = pl.ds(pl.multiple_of(me * block, block), block)

    barrier = pltpu.get_barrier_semaphore()

    @pl.loop(1, n)
    def _(k):
        pl.semaphore_signal(barrier, inc=1, device_id={"seq": lax.rem(me + k, n)}, device_id_type=MESH)

    @pl.loop(1, tps)
    def _(k):
        pl.semaphore_signal(barrier, inc=1, device_id={"tp": lax.rem(tp + k, tps)}, device_id_type=MESH)

    pl.semaphore_wait(barrier, n + tps - 2)

    def send(phase, g, src, dst, to):
        pltpu.make_async_remote_copy(
            src_ref=src, dst_ref=dst, send_sem=send_sem.at[phase, g], recv_sem=recv_sem.at[phase, g],
            device_id={"seq": to}, device_id_type=MESH,
        ).start()

    def wait(sem, phase, g, buffer):
        some = buffer.at[pl.ds(0, n - 1)]
        pltpu.make_async_copy(some, some, sem.at[phase, g]).wait()

    def wait_rows(sem, phase, g, buffer):
        some = buffer.at[pl.ds(0, (n - 1) * block)]
        pltpu.make_async_copy(some, some, sem.at[phase, g]).wait()

    local = {}
    for g in range(quads):
        columns = pl.ds(g * QUAD, QUAD)
        local[g] = (
            pltpu.make_async_copy(group_ref.at[0, 0, my_rows, columns], spread[g].at[me], local_sem.at[0, g]),
            pltpu.make_async_copy(group_ref.at[:, 0, :, columns], own.at[g], local_sem.at[1, g]),
            pltpu.make_async_copy(
                cache_ref.at[:, 0, :, pl.ds(pl.multiple_of(tp * width + g * QUAD, LANES), QUAD)],
                kv.at[g, :, pl.ds(pl.multiple_of(tp * positions, positions), positions)],
                local_sem.at[2, g],
            ),
        )

        @pl.loop(1, n)
        def _(k):
            to = lax.rem(me + k, n)
            send(
                0, g, group_ref.at[0, 0, pl.ds(pl.multiple_of(to * block, block), block), columns],
                spread[g].at[me], to,
            )

        local[g][0].start()

        @pl.loop(1, tps)
        def _(k):
            to = lax.rem(tp + k, tps)
            pltpu.make_async_remote_copy(
                src_ref=cache_ref.at[:, 0, :, pl.ds(pl.multiple_of(to * width + g * QUAD, LANES), QUAD)],
                dst_ref=kv.at[g, :, pl.ds(pl.multiple_of(tp * positions, positions), positions)],
                send_sem=kv_send.at[g], recv_sem=kv_recv.at[g], device_id={"tp": to}, device_id_type=MESH,
            ).start()

        local[g][1].start()
        local[g][2].start()

    lane = lax.broadcasted_iota(jnp.int32, (1, LANES), 1)
    causal = lax.broadcasted_iota(jnp.int32, (rows, rows), 0) >= lax.broadcasted_iota(jnp.int32, (rows, rows), 1)

    own_log[...] = jnp.zeros_like(own_log)
    for g in range(quads):
        wait(recv_sem, 0, g, spread[g])
        local[g][0].wait()

        asked[g][my_rows, :] = spread[g][source_ref[me]]

        @pl.loop(1, n)
        def _(k):
            to = lax.rem(me + k, n)
            staged[g][to] = spread[g][source_ref[to]]
            send(1, g, staged[g].at[to], asked[g].at[my_rows], to)

        local[g][1].wait()
        tiles, logs = attend_quad(
            lambda s, w: own[g, 0, :, s : s + w],
            lambda s, w: own[g, 1, :, s : s + w],
            lambda s, w: own[g, 2, :, s : s + w],
            causal,
        )
        for i, tile in enumerate(tiles):
            own_mix[:, g * QUAD + i * LANES : g * QUAD + (i + 1) * LANES] = tile
        for i, log in enumerate(logs):
            own_log[...] = jnp.where(lane == g * 4 + i, log, own_log[...])

    live = lax.broadcasted_iota(jnp.int32, (1, tps * positions), 1) < length_ref[0]
    old_log[...] = jnp.zeros_like(old_log)
    for g in range(quads):
        wait_rows(recv_sem, 1, g, asked[g])
        local[g][2].wait()
        arrived = kv.at[g, :, pl.ds(0, (tps - 1) * positions)]
        pltpu.make_async_copy(arrived, arrived, kv_recv.at[g]).wait()
        tiles, logs = attend_quad(
            lambda s, w: asked[g][:, s : s + w],
            lambda s, w: kv[g, 0, :, s : s + w],
            lambda s, w: kv[g, 1, :, s : s + w],
            live,
        )
        for i, tile in enumerate(tiles):
            partial[g][:, i * LANES : (i + 1) * LANES] = tile.astype(jnp.bfloat16)
        for i, log in enumerate(logs):
            old_log[...] = jnp.where(lax.rem(lane, heads) == g * 4 + i, log, old_log[...])
        if g == quads - 1:
            log = old_log[...]
            high = log.astype(jnp.bfloat16).astype(jnp.float32)
            middle = (log - high).astype(jnp.bfloat16).astype(jnp.float32)
            low = log - high - middle
            pieces = jnp.where(lane < heads, high, jnp.where(lane < 2 * heads, middle, low))
            partial[g][:, QUAD:] = pieces.astype(jnp.bfloat16)

        landed[g][me] = partial[g][my_rows, :]

        @pl.loop(1, n)
        def _(k):
            to = lax.rem(me + k, n)
            send(
                2, g, partial[g].at[pl.ds(pl.multiple_of(to * block, block), block)], landed[g].at[me], to
            )

    for g in range(quads):
        wait(recv_sem, 2, g, landed[g])
        answer[g][my_rows, :] = landed[g][slot_ref[me]]

        @pl.loop(1, n)
        def _(k):
            to = lax.rem(me + k, n)
            restaged[g][to] = landed[g][slot_ref[to]]
            send(3, g, restaged[g].at[to], answer[g].at[my_rows], to)

    for g in range(quads):
        wait_rows(recv_sem, 3, g, answer[g])
    pieces = answer[quads - 1][:, QUAD:].astype(jnp.float32)
    log = pieces + pltpu.roll(pieces, LANES - heads, 1) + pltpu.roll(pieces, LANES - 2 * heads, 1)
    share = 1.0 / (1.0 + jnp.exp(own_log[...] - log))
    for g in range(quads):
        parts = [share[:, g * 4 + i : g * 4 + i + 1] for i in range(4)]
        for i, (edge, left, right) in enumerate(((96, 0, 1), (64, 1, 2), (32, 2, 3))):
            portion = jnp.where(lane < edge, parts[left], parts[right])
            columns = slice(g * QUAD + i * LANES, g * QUAD + (i + 1) * LANES)
            mine = own_mix[:, columns]
            theirs = answer[g][:, i * LANES : (i + 1) * LANES].astype(jnp.float32)
            out_ref[0, :, columns] = (mine + portion * (theirs - mine)).astype(jnp.bfloat16)

    for g in range(quads):
        wait(send_sem, 0, g, spread[g])
        wait(send_sem, 1, g, staged[g])
        wait(send_sem, 2, g, landed[g])
        wait(send_sem, 3, g, restaged[g])
        sent = kv.at[g, :, pl.ds(0, (tps - 1) * positions)]
        pltpu.make_async_copy(sent, sent, kv_send.at[g]).wait()


def fused(n, tps, cache, cache_len, group, group_req, req_order):
    slot_of = inverse_table(req_order)
    index_of = inverse_table(group_req)
    slot_for_index = small_take(slot_of, group_req)
    index_for_slot = small_take(index_of, req_order)
    my_request = small_take(req_order, lax.axis_index("seq")[None])
    length = small_take(cache_len, my_request)
    rows, width = group.shape[2], group.shape[3]
    positions = cache.shape[2]
    quads = width // QUAD
    block = rows // n
    widths = [QUAD] * (quads - 1) + [QUAD + LANES]

    def blocks(sizes):
        return [pltpu.VMEM((n, block, w), jnp.bfloat16) for w in sizes]

    def whole(sizes):
        return [pltpu.VMEM((rows, w), jnp.bfloat16) for w in sizes]

    plain = [QUAD] * quads
    return pl.pallas_call(
        functools.partial(kernel, n, tps, quads),
        out_shape=jax.ShapeDtypeStruct((1, rows, width), jnp.bfloat16),
        in_specs=[pl.BlockSpec(memory_space=pltpu.SMEM)] * 3 + [pl.BlockSpec(memory_space=pl.ANY)] * 2,
        out_specs=pl.BlockSpec(memory_space=pltpu.VMEM),
        scratch_shapes=[
            pltpu.VMEM((quads, 2, tps * positions, QUAD), jnp.bfloat16),
            pltpu.VMEM((quads, 3, rows, QUAD), jnp.bfloat16),
            pltpu.VMEM((rows, width), jnp.float32),
            pltpu.VMEM((rows, LANES), jnp.float32),
            pltpu.VMEM((rows, LANES), jnp.float32),
            *blocks(plain), *blocks(plain), *whole(plain), *whole(widths),
            *blocks(widths), *blocks(widths), *whole(widths),
            pltpu.SemaphoreType.DMA((4, quads)),
            pltpu.SemaphoreType.DMA((4, quads)),
            pltpu.SemaphoreType.DMA((quads,)),
            pltpu.SemaphoreType.DMA((quads,)),
            pltpu.SemaphoreType.DMA((3, quads)),
        ],
        compiler_params=pltpu.CompilerParams(
            collective_id=0, has_side_effects=True, vmem_limit_bytes=48 * 2**20
        ),
        cost_estimate=pl.CostEstimate(
            flops=4 * rows * width * (rows + tps * positions),
            bytes_accessed=cache.size * 2 + group.size * 2,
            transcendentals=rows * (rows + tps * positions) * width // HD,
        ),
    )(index_for_slot, slot_for_index, length, cache, group)


def small_take(table, index):
    hits = index[:, None] == jnp.arange(table.shape[0], dtype=jnp.int32)[None, :]
    return jnp.sum(jnp.where(hits, table[None, :], 0), axis=1)


def pick(array, index):
    return jnp.stack(
        [lax.dynamic_index_in_dim(array, index[i], 1, keepdims=False) for i in range(array.shape[1])], axis=1
    )


def inverse_table(permutation):
    numbers = jnp.arange(permutation.shape[0], dtype=jnp.int32)
    matches = permutation[None, :] == numbers[:, None]
    return jnp.sum(jnp.where(matches, numbers[None, :], 0), axis=1)


def online_part(queries, key_rows, value_rows, keep_rows, block_rows, block_count, factor):
    row_count = queries.shape[0]
    head_count = queries.shape[1]

    def add_block(block_index, carry):
        row_top, weight_sum, weighted = carry
        block_start = block_index * block_rows
        scores = (
            jnp.einsum("qhd,khd->hqk", queries, key_rows, preferred_element_type=jnp.float32)
            * factor
        )
        scores = jnp.where(keep_rows(block_start)[None], scores, -jnp.inf)
        new_top = jnp.maximum(row_top, jnp.max(scores, axis=-1))
        rescale = jnp.exp(row_top - new_top)
        weights = jnp.exp(scores - new_top[..., None]).astype(jnp.bfloat16)
        weight_sum = weight_sum * rescale + jnp.sum(weights, axis=-1, dtype=jnp.float32)
        weighted = weighted * rescale[..., None] + jnp.einsum(
            "hqk,khd->hqd", weights, value_rows, preferred_element_type=jnp.float32
        )
        return (new_top, weight_sum, weighted)

    start_top = jnp.full((head_count, row_count), -jnp.inf, jnp.float32)
    start_sum = jnp.zeros((head_count, row_count), jnp.float32)
    start_mixed = jnp.zeros((head_count, row_count, queries.shape[2]), jnp.float32)
    return lax.fori_loop(0, block_count, add_block, (start_top, start_sum, start_mixed))


def combine_parts(first_part, second_part):
    top_one, sum_one, mixed_one = first_part
    top_two, sum_two, mixed_two = second_part
    row_top = jnp.maximum(top_one, top_two)
    factor_one = jnp.exp(top_one - row_top)
    factor_two = jnp.exp(top_two - row_top)
    result = (factor_one[..., None] * mixed_one + factor_two[..., None] * mixed_two) / (
        factor_one * sum_one + factor_two * sum_two
    )[..., None]
    result = jnp.transpose(result, (1, 0, 2))
    return result.reshape(result.shape[0], -1).astype(jnp.bfloat16)


def shards(cache, cache_len, group, group_req, req_order):
    factor = 1.0 / math.sqrt(HD)
    slot_of = inverse_table(req_order)
    source_slot = jnp.take(slot_of, group_req)
    my_request = jnp.take(group_req, lax.axis_index("seq"))
    length = jnp.take(cache_len, my_request)
    row_count = group.shape[2]
    head_count = group.shape[3] // HD
    queries = group[0, 0].reshape(row_count, head_count, HD)
    new_keys = group[1, 0].reshape(row_count, head_count, HD)
    new_values = group[2, 0].reshape(row_count, head_count, HD)
    group_block = min(512, row_count)

    def causal_rows(block_start):
        key_index = block_start + jnp.arange(group_block, dtype=jnp.int32)
        return jnp.arange(row_count, dtype=jnp.int32)[:, None] >= key_index[None, :]

    group_part = online_part(
        queries, new_keys, new_values, causal_rows, group_block, row_count // group_block, factor
    )
    spread = lax.all_to_all(cache, "seq", split_axis=2, concat_axis=1, tiled=True)
    ordered = pick(spread, source_slot)
    moved = lax.all_to_all(
        lax.all_to_all(ordered, "seq", split_axis=1, concat_axis=2, tiled=True),
        "tp",
        split_axis=3,
        concat_axis=2,
        tiled=True,
    )
    position_count = moved.shape[2]
    old_keys = moved[0, 0].reshape(position_count, head_count, HD)
    old_values = moved[1, 0].reshape(position_count, head_count, HD)
    cache_block = min(512, position_count)

    def live_rows(block_start):
        positions = block_start + jnp.arange(cache_block, dtype=jnp.int32)
        return (positions < length)[None, :]

    block_total = position_count // cache_block
    cache_part = online_part(
        queries, old_keys, old_values, live_rows, cache_block, block_total, factor
    )
    context = combine_parts(cache_part, group_part)
    return context[None]


def solution(mesh):
    n, tps = mesh.shape["seq"], mesh.shape["tp"]

    def run(cache, cache_len, group, group_req, req_order):
        rows, width = group.shape[2], group.shape[3]
        whole_blocks = rows % (16 * n) == 0 and width % QUAD == 0 and 3 * (width // HD) <= LANES
        if whole_blocks and tps > 1 and cache.shape[2] % 16 == 0:
            return fused(n, tps, cache, cache_len, group, group_req, req_order)
        return shards(cache, cache_len, group, group_req, req_order)

    in_specs = (P(None, "seq", "tp", None), P(), P(None, "seq", None, "tp"), P(), P())
    out_specs = P("seq", None, "tp")
    return jax.shard_map(run, mesh=mesh, in_specs=in_specs, out_specs=out_specs, check_vma=False)
```

```python
import functools
import math

import jax
import jax.numpy as jnp
from jax import lax
from jax.experimental import pallas as pl
from jax.experimental.pallas import tpu as pltpu
from jax.sharding import PartitionSpec as P

HD = 96
QUAD = 4 * HD
LANES = 128
MESH = pl.DeviceIdType.MESH
FACTOR = 1.0 / math.sqrt(HD)
WINDOWS = ((0, 128, 0), (0, 256, 96), (128, 256, 64), (256, 128, 32))


def attend(queries, key_rows, value_rows, keep, first_lane):
    width = queries.shape[1]
    lane = lax.broadcasted_iota(jnp.int32, (1, width), 1)
    mine = jnp.where((lane >= first_lane) & (lane < first_lane + HD), 1.0, 0.0)
    mask = mine.astype(jnp.bfloat16)
    rest = (1.0 - mine).astype(jnp.bfloat16)
    scores = lax.dot_general(
        queries * mask, key_rows, (((1,), (1,)), ((), ())), preferred_element_type=jnp.float32
    )
    scores = jnp.where(keep, scores, -jnp.inf)
    top = jnp.max(scores, axis=1, keepdims=True)
    weights = jnp.exp((scores - top) * FACTOR).astype(jnp.bfloat16)
    mixed = jnp.dot(weights, value_rows * mask + rest, preferred_element_type=jnp.float32)
    free = 0 if first_lane > 0 else HD
    total = mixed[:, free : free + 1]
    return mixed * (1.0 / total), top * FACTOR + jnp.log(total)


def attend_quad(load_queries, load_keys, load_values, keep):
    parts, logs = [], []
    for start, width, first_lane in WINDOWS:
        mix, log = attend(
            load_queries(start, width), load_keys(start, width), load_values(start, width), keep, first_lane
        )
        parts.append(mix)
        logs.append(log)
    lane = lax.broadcasted_iota(jnp.int32, (1, LANES), 1)
    tiles = (
        jnp.where(lane < 96, parts[0], parts[1][:, :LANES]),
        jnp.where(lane < 64, parts[1][:, LANES:], parts[2][:, :LANES]),
        jnp.where(lane < 32, parts[2][:, LANES:], parts[3]),
    )
    return tiles, logs


def kernel(
    n, tps, quads, length_any, request_any, order_any, cache_ref, group_ref, out_ref,
    length_ref, request_ref, order_ref, source_ref, slot_ref, kv, own, own_mix, own_log, old_log, *rest,
):
    spread, staged, asked, partial, landed, restaged, answer = (
        rest[i * quads : (i + 1) * quads] for i in range(7)
    )
    send_sem, recv_sem, kv_send, kv_recv, local_sem, table_sem = rest[7 * quads :]
    me, tp = lax.axis_index("seq"), lax.axis_index("tp")
    rows = group_ref.shape[2]
    block = rows // n
    width = group_ref.shape[3]
    heads = width // HD
    positions = cache_ref.shape[2]
    my_rows = pl.ds(pl.multiple_of(me * block, block), block)

    barrier = pltpu.get_barrier_semaphore()

    @pl.loop(1, n)
    def _(k):
        pl.semaphore_signal(barrier, inc=1, device_id={"seq": lax.rem(me + k, n)}, device_id_type=MESH)

    @pl.loop(1, tps)
    def _(k):
        pl.semaphore_signal(barrier, inc=1, device_id={"tp": lax.rem(tp + k, tps)}, device_id_type=MESH)

    tables = [
        pltpu.make_async_copy(array, table, table_sem.at[i])
        for i, (array, table) in enumerate(
            ((length_any, length_ref), (request_any, request_ref), (order_any, order_ref))
        )
    ]
    for copy in tables:
        copy.start()
    local = {}
    for g in range(quads):
        columns = pl.ds(g * QUAD, QUAD)
        local[g] = (
            pltpu.make_async_copy(group_ref.at[0, 0, my_rows, columns], spread[g].at[me], local_sem.at[0, g]),
            pltpu.make_async_copy(group_ref.at[:, 0, :, columns], own.at[g], local_sem.at[1, g]),
            pltpu.make_async_copy(
                cache_ref.at[:, 0, :, pl.ds(pl.multiple_of(tp * width + g * QUAD, LANES), QUAD)],
                kv.at[g, :, pl.ds(pl.multiple_of(tp * positions, positions), positions)],
                local_sem.at[2, g],
            ),
        )
        for copy in local[g]:
            copy.start()

    pl.semaphore_wait(barrier, n + tps - 2)

    def send(phase, g, src, dst, to):
        pltpu.make_async_remote_copy(
            src_ref=src, dst_ref=dst, send_sem=send_sem.at[phase, g], recv_sem=recv_sem.at[phase, g],
            device_id={"seq": to}, device_id_type=MESH,
        ).start()

    def wait(sem, phase, g, buffer):
        some = buffer.at[pl.ds(0, n - 1)]
        pltpu.make_async_copy(some, some, sem.at[phase, g]).wait()

    def wait_rows(sem, phase, g, buffer):
        some = buffer.at[pl.ds(0, (n - 1) * block)]
        pltpu.make_async_copy(some, some, sem.at[phase, g]).wait()

    for g in range(quads):
        columns = pl.ds(g * QUAD, QUAD)

        @pl.loop(1, n)
        def _(k):
            to = lax.rem(me + k, n)
            send(
                0, g, group_ref.at[0, 0, pl.ds(pl.multiple_of(to * block, block), block), columns],
                spread[g].at[me], to,
            )

        @pl.loop(1, tps)
        def _(k):
            to = lax.rem(tp + k, tps)
            pltpu.make_async_remote_copy(
                src_ref=cache_ref.at[:, 0, :, pl.ds(pl.multiple_of(to * width + g * QUAD, LANES), QUAD)],
                dst_ref=kv.at[g, :, pl.ds(pl.multiple_of(tp * positions, positions), positions)],
                send_sem=kv_send.at[g], recv_sem=kv_recv.at[g], device_id={"tp": to}, device_id_type=MESH,
            ).start()


    for copy in tables:
        copy.wait()

    @pl.loop(0, n)
    def _(i):
        source, slot = jnp.int32(0), jnp.int32(0)
        for j in range(n):
            source = jnp.maximum(source, jnp.where(request_ref[j] == order_ref[i], j, 0))
            slot = jnp.maximum(slot, jnp.where(order_ref[j] == request_ref[i], j, 0))
        source_ref[i] = source
        slot_ref[i] = slot

    lane = lax.broadcasted_iota(jnp.int32, (1, LANES), 1)
    causal = lax.broadcasted_iota(jnp.int32, (rows, rows), 0) >= lax.broadcasted_iota(jnp.int32, (rows, rows), 1)

    own_log[...] = jnp.zeros_like(own_log)
    for g in range(quads):
        wait(recv_sem, 0, g, spread[g])
        local[g][0].wait()

        asked[g][my_rows, :] = spread[g][source_ref[me]]

        @pl.loop(1, n)
        def _(k):
            to = lax.rem(me + k, n)
            staged[g][to] = spread[g][source_ref[to]]
            send(1, g, staged[g].at[to], asked[g].at[my_rows], to)

    for g in range(quads):
        local[g][1].wait()
        tiles, logs = attend_quad(
            lambda s, w: own[g, 0, :, s : s + w],
            lambda s, w: own[g, 1, :, s : s + w],
            lambda s, w: own[g, 2, :, s : s + w],
            causal,
        )
        for i, tile in enumerate(tiles):
            own_mix[:, g * QUAD + i * LANES : g * QUAD + (i + 1) * LANES] = tile
        for i, log in enumerate(logs):
            own_log[...] = jnp.where(lane == g * 4 + i, log, own_log[...])

    def relay(g):
        wait(recv_sem, 2, g, landed[g])
        answer[g][my_rows, :] = landed[g][slot_ref[me]]

        @pl.loop(1, n)
        def _(k):
            to = lax.rem(me + k, n)
            restaged[g][to] = landed[g][slot_ref[to]]
            send(3, g, restaged[g].at[to], answer[g].at[my_rows], to)

    live = lax.broadcasted_iota(jnp.int32, (1, tps * positions), 1) < length_ref[order_ref[me]]
    old_log[...] = jnp.zeros_like(old_log)
    for g in range(quads):
        wait_rows(recv_sem, 1, g, asked[g])
        local[g][2].wait()
        arrived = kv.at[g, :, pl.ds(0, (tps - 1) * positions)]
        pltpu.make_async_copy(arrived, arrived, kv_recv.at[g]).wait()
        tiles, logs = attend_quad(
            lambda s, w: asked[g][:, s : s + w],
            lambda s, w: kv[g, 0, :, s : s + w],
            lambda s, w: kv[g, 1, :, s : s + w],
            live,
        )
        for i, tile in enumerate(tiles):
            partial[g][:, i * LANES : (i + 1) * LANES] = tile.astype(jnp.bfloat16)
        for i, log in enumerate(logs):
            old_log[...] = jnp.where(lax.rem(lane, heads) == g * 4 + i, log, old_log[...])
        if g == quads - 1:
            log = old_log[...]
            high = log.astype(jnp.bfloat16).astype(jnp.float32)
            middle = (log - high).astype(jnp.bfloat16).astype(jnp.float32)
            low = log - high - middle
            pieces = jnp.where(lane < heads, high, jnp.where(lane < 2 * heads, middle, low))
            partial[g][:, QUAD:] = pieces.astype(jnp.bfloat16)

        landed[g][me] = partial[g][my_rows, :]

        @pl.loop(1, n)
        def _(k):
            to = lax.rem(me + k, n)
            send(
                2, g, partial[g].at[pl.ds(pl.multiple_of(to * block, block), block)], landed[g].at[me], to
            )

        if g >= 2:
            relay(g - 2)

    for g in range(max(quads - 2, 0), quads):
        relay(g)

    for g in range(quads):
        wait_rows(recv_sem, 3, g, answer[g])
    pieces = answer[quads - 1][:, QUAD:].astype(jnp.float32)
    log = pieces + pltpu.roll(pieces, LANES - heads, 1) + pltpu.roll(pieces, LANES - 2 * heads, 1)
    share = 1.0 / (1.0 + jnp.exp(own_log[...] - log))
    for g in range(quads):
        parts = [share[:, g * 4 + i : g * 4 + i + 1] for i in range(4)]
        for i, (edge, left, right) in enumerate(((96, 0, 1), (64, 1, 2), (32, 2, 3))):
            portion = jnp.where(lane < edge, parts[left], parts[right])
            columns = slice(g * QUAD + i * LANES, g * QUAD + (i + 1) * LANES)
            mine = own_mix[:, columns]
            theirs = answer[g][:, i * LANES : (i + 1) * LANES].astype(jnp.float32)
            out_ref[0, :, columns] = (mine + portion * (theirs - mine)).astype(jnp.bfloat16)

    for g in range(quads):
        wait(send_sem, 0, g, spread[g])
        wait(send_sem, 1, g, staged[g])
        wait(send_sem, 2, g, landed[g])
        wait(send_sem, 3, g, restaged[g])
        sent = kv.at[g, :, pl.ds(0, (tps - 1) * positions)]
        pltpu.make_async_copy(sent, sent, kv_send.at[g]).wait()


def fused(n, tps, cache, cache_len, group, group_req, req_order):
    rows, width = group.shape[2], group.shape[3]
    positions = cache.shape[2]
    quads = width // QUAD
    block = rows // n
    widths = [QUAD] * (quads - 1) + [QUAD + LANES]

    def blocks(sizes):
        return [pltpu.VMEM((n, block, w), jnp.bfloat16) for w in sizes]

    def whole(sizes):
        return [pltpu.VMEM((rows, w), jnp.bfloat16) for w in sizes]

    plain = [QUAD] * quads
    return pl.pallas_call(
        functools.partial(kernel, n, tps, quads),
        out_shape=jax.ShapeDtypeStruct((1, rows, width), jnp.bfloat16),
        in_specs=[pl.BlockSpec(memory_space=pl.ANY)] * 5,
        out_specs=pl.BlockSpec(memory_space=pltpu.VMEM),
        scratch_shapes=[
            *[pltpu.SMEM((n,), jnp.int32)] * 5,
            pltpu.VMEM((quads, 2, tps * positions, QUAD), jnp.bfloat16),
            pltpu.VMEM((quads, 3, rows, QUAD), jnp.bfloat16),
            pltpu.VMEM((rows, width), jnp.float32),
            pltpu.VMEM((rows, LANES), jnp.float32),
            pltpu.VMEM((rows, LANES), jnp.float32),
            *blocks(plain), *blocks(plain), *whole(plain), *whole(widths),
            *blocks(widths), *blocks(widths), *whole(widths),
            pltpu.SemaphoreType.DMA((4, quads)),
            pltpu.SemaphoreType.DMA((4, quads)),
            pltpu.SemaphoreType.DMA((quads,)),
            pltpu.SemaphoreType.DMA((quads,)),
            pltpu.SemaphoreType.DMA((3, quads)),
            pltpu.SemaphoreType.DMA((3,)),
        ],
        compiler_params=pltpu.CompilerParams(
            collective_id=0, has_side_effects=True, vmem_limit_bytes=59 * 2**20
        ),
        cost_estimate=pl.CostEstimate(
            flops=4 * rows * width * (rows + tps * positions),
            bytes_accessed=cache.size * 2 + group.size * 2,
            transcendentals=rows * (rows + tps * positions) * width // HD,
        ),
    )(cache_len, group_req, req_order, cache, group)


def pick(array, index):
    return jnp.stack(
        [lax.dynamic_index_in_dim(array, index[i], 1, keepdims=False) for i in range(array.shape[1])], axis=1
    )


def inverse_table(permutation):
    numbers = jnp.arange(permutation.shape[0], dtype=jnp.int32)
    matches = permutation[None, :] == numbers[:, None]
    return jnp.sum(jnp.where(matches, numbers[None, :], 0), axis=1)


def online_part(queries, key_rows, value_rows, keep_rows, block_rows, block_count, factor):
    row_count = queries.shape[0]
    head_count = queries.shape[1]

    def add_block(block_index, carry):
        row_top, weight_sum, weighted = carry
        block_start = block_index * block_rows
        scores = (
            jnp.einsum("qhd,khd->hqk", queries, key_rows, preferred_element_type=jnp.float32)
            * factor
        )
        scores = jnp.where(keep_rows(block_start)[None], scores, -jnp.inf)
        new_top = jnp.maximum(row_top, jnp.max(scores, axis=-1))
        rescale = jnp.exp(row_top - new_top)
        weights = jnp.exp(scores - new_top[..., None]).astype(jnp.bfloat16)
        weight_sum = weight_sum * rescale + jnp.sum(weights, axis=-1, dtype=jnp.float32)
        weighted = weighted * rescale[..., None] + jnp.einsum(
            "hqk,khd->hqd", weights, value_rows, preferred_element_type=jnp.float32
        )
        return (new_top, weight_sum, weighted)

    start_top = jnp.full((head_count, row_count), -jnp.inf, jnp.float32)
    start_sum = jnp.zeros((head_count, row_count), jnp.float32)
    start_mixed = jnp.zeros((head_count, row_count, queries.shape[2]), jnp.float32)
    return lax.fori_loop(0, block_count, add_block, (start_top, start_sum, start_mixed))


def combine_parts(first_part, second_part):
    top_one, sum_one, mixed_one = first_part
    top_two, sum_two, mixed_two = second_part
    row_top = jnp.maximum(top_one, top_two)
    factor_one = jnp.exp(top_one - row_top)
    factor_two = jnp.exp(top_two - row_top)
    result = (factor_one[..., None] * mixed_one + factor_two[..., None] * mixed_two) / (
        factor_one * sum_one + factor_two * sum_two
    )[..., None]
    result = jnp.transpose(result, (1, 0, 2))
    return result.reshape(result.shape[0], -1).astype(jnp.bfloat16)


def shards(cache, cache_len, group, group_req, req_order):
    factor = 1.0 / math.sqrt(HD)
    slot_of = inverse_table(req_order)
    source_slot = jnp.take(slot_of, group_req)
    my_request = jnp.take(group_req, lax.axis_index("seq"))
    length = jnp.take(cache_len, my_request)
    row_count = group.shape[2]
    head_count = group.shape[3] // HD
    queries = group[0, 0].reshape(row_count, head_count, HD)
    new_keys = group[1, 0].reshape(row_count, head_count, HD)
    new_values = group[2, 0].reshape(row_count, head_count, HD)
    group_block = min(512, row_count)

    def causal_rows(block_start):
        key_index = block_start + jnp.arange(group_block, dtype=jnp.int32)
        return jnp.arange(row_count, dtype=jnp.int32)[:, None] >= key_index[None, :]

    group_part = online_part(
        queries, new_keys, new_values, causal_rows, group_block, row_count // group_block, factor
    )
    spread = lax.all_to_all(cache, "seq", split_axis=2, concat_axis=1, tiled=True)
    ordered = pick(spread, source_slot)
    moved = lax.all_to_all(
        lax.all_to_all(ordered, "seq", split_axis=1, concat_axis=2, tiled=True),
        "tp",
        split_axis=3,
        concat_axis=2,
        tiled=True,
    )
    position_count = moved.shape[2]
    old_keys = moved[0, 0].reshape(position_count, head_count, HD)
    old_values = moved[1, 0].reshape(position_count, head_count, HD)
    cache_block = min(512, position_count)

    def live_rows(block_start):
        positions = block_start + jnp.arange(cache_block, dtype=jnp.int32)
        return (positions < length)[None, :]

    block_total = position_count // cache_block
    cache_part = online_part(
        queries, old_keys, old_values, live_rows, cache_block, block_total, factor
    )
    context = combine_parts(cache_part, group_part)
    return context[None]


def solution(mesh):
    n, tps = mesh.shape["seq"], mesh.shape["tp"]

    def run(cache, cache_len, group, group_req, req_order):
        rows, width = group.shape[2], group.shape[3]
        whole_blocks = rows % (16 * n) == 0 and width % QUAD == 0 and 3 * (width // HD) <= LANES
        if whole_blocks and tps > 1 and cache.shape[2] % 16 == 0:
            return fused(n, tps, cache, cache_len, group, group_req, req_order)
        return shards(cache, cache_len, group, group_req, req_order)

    in_specs = (P(None, "seq", "tp", None), P(), P(None, "seq", None, "tp"), P(), P())
    out_specs = P("seq", None, "tp")
    return jax.shard_map(run, mesh=mesh, in_specs=in_specs, out_specs=out_specs, check_vma=False)
```

```python
import functools
import math

import jax
import jax.numpy as jnp
from jax import lax
from jax.experimental import pallas as pl
from jax.experimental.pallas import tpu as pltpu
from jax.sharding import PartitionSpec as P

HD = 96
QUAD = 4 * HD
LANES = 128
MESH = pl.DeviceIdType.MESH
FACTOR = 1.0 / math.sqrt(HD)
WINDOWS = ((0, 128, 0), (0, 256, 96), (128, 256, 64), (256, 128, 32))


def attend(queries, key_rows, value_rows, keep, first_lane):
    width = queries.shape[1]
    lane = lax.broadcasted_iota(jnp.int32, (1, width), 1)
    mine = jnp.where((lane >= first_lane) & (lane < first_lane + HD), 1.0, 0.0)
    mask = mine.astype(jnp.bfloat16)
    rest = (1.0 - mine).astype(jnp.bfloat16)
    scores = lax.dot_general(
        queries * mask, key_rows, (((1,), (1,)), ((), ())), preferred_element_type=jnp.float32
    )
    scores = jnp.where(keep, scores, -jnp.inf)
    top = jnp.max(scores, axis=1, keepdims=True)
    weights = jnp.exp((scores - top) * FACTOR).astype(jnp.bfloat16)
    mixed = jnp.dot(weights, value_rows * mask + rest, preferred_element_type=jnp.float32)
    free = 0 if first_lane > 0 else HD
    total = mixed[:, free : free + 1]
    return mixed * (1.0 / total), top * FACTOR + jnp.log(total)


def attend_quad(load_queries, load_keys, load_values, keep):
    parts, logs = [], []
    for start, width, first_lane in WINDOWS:
        mix, log = attend(
            load_queries(start, width), load_keys(start, width), load_values(start, width), keep, first_lane
        )
        parts.append(mix)
        logs.append(log)
    lane = lax.broadcasted_iota(jnp.int32, (1, LANES), 1)
    tiles = (
        jnp.where(lane < 96, parts[0], parts[1][:, :LANES]),
        jnp.where(lane < 64, parts[1][:, LANES:], parts[2][:, :LANES]),
        jnp.where(lane < 32, parts[2][:, LANES:], parts[3]),
    )
    return tiles, logs


def kernel(
    n, tps, quads, tables_any, cache_ref, group_ref, out_ref,
    tables_ref, source_ref, slot_ref, kv, own, own_mix, own_log, old_log, *rest,
):
    spread, staged, asked, partial, landed, restaged, answer = (
        rest[i * quads : (i + 1) * quads] for i in range(7)
    )
    send_sem, recv_sem, kv_send, kv_recv, local_sem, table_sem = rest[7 * quads :]
    me, tp = lax.axis_index("seq"), lax.axis_index("tp")
    rows = group_ref.shape[2]
    block = rows // n
    width = group_ref.shape[3]
    heads = width // HD
    positions = cache_ref.shape[2]
    my_rows = pl.ds(pl.multiple_of(me * block, block), block)

    barrier = pltpu.get_barrier_semaphore()

    @pl.loop(1, n)
    def _(k):
        pl.semaphore_signal(barrier, inc=1, device_id={"seq": lax.rem(me + k, n)}, device_id_type=MESH)

    @pl.loop(1, tps)
    def _(k):
        pl.semaphore_signal(barrier, inc=1, device_id={"tp": lax.rem(tp + k, tps)}, device_id_type=MESH)

    tables = [pltpu.make_async_copy(tables_any, tables_ref, table_sem.at[0])]
    for copy in tables:
        copy.start()
    local = {}
    for g in range(quads):
        columns = pl.ds(g * QUAD, QUAD)
        local[g] = (
            pltpu.make_async_copy(group_ref.at[0, 0, my_rows, columns], spread[g].at[me], local_sem.at[0, g]),
            pltpu.make_async_copy(group_ref.at[:, 0, :, columns], own.at[g], local_sem.at[1, g]),
            pltpu.make_async_copy(
                cache_ref.at[:, 0, :, pl.ds(pl.multiple_of(tp * width + g * QUAD, LANES), QUAD)],
                kv.at[g, :, pl.ds(pl.multiple_of(tp * positions, positions), positions)],
                local_sem.at[2, g],
            ),
        )
        for copy in local[g]:
            copy.start()

    pl.semaphore_wait(barrier, n + tps - 2)

    def send(phase, g, src, dst, to):
        pltpu.make_async_remote_copy(
            src_ref=src, dst_ref=dst, send_sem=send_sem.at[phase, g], recv_sem=recv_sem.at[phase, g],
            device_id={"seq": to}, device_id_type=MESH,
        ).start()

    def wait(sem, phase, g, buffer):
        some = buffer.at[pl.ds(0, n - 1)]
        pltpu.make_async_copy(some, some, sem.at[phase, g]).wait()

    def wait_rows(sem, phase, g, buffer):
        some = buffer.at[pl.ds(0, (n - 1) * block)]
        pltpu.make_async_copy(some, some, sem.at[phase, g]).wait()

    for g in range(quads):
        columns = pl.ds(g * QUAD, QUAD)

        @pl.loop(1, n)
        def _(k):
            to = lax.rem(me + k, n)
            send(
                0, g, group_ref.at[0, 0, pl.ds(pl.multiple_of(to * block, block), block), columns],
                spread[g].at[me], to,
            )

        @pl.loop(1, tps)
        def _(k):
            to = lax.rem(tp + k, tps)
            pltpu.make_async_remote_copy(
                src_ref=cache_ref.at[:, 0, :, pl.ds(pl.multiple_of(to * width + g * QUAD, LANES), QUAD)],
                dst_ref=kv.at[g, :, pl.ds(pl.multiple_of(tp * positions, positions), positions)],
                send_sem=kv_send.at[g], recv_sem=kv_recv.at[g], device_id={"tp": to}, device_id_type=MESH,
            ).start()


    for copy in tables:
        copy.wait()

    @pl.loop(0, n)
    def _(i):
        source, slot = jnp.int32(0), jnp.int32(0)
        for j in range(n):
            source = jnp.maximum(source, jnp.where(tables_ref[n + j] == tables_ref[2 * n + i], j, 0))
            slot = jnp.maximum(slot, jnp.where(tables_ref[2 * n + j] == tables_ref[n + i], j, 0))
        source_ref[i] = source
        slot_ref[i] = slot

    lane = lax.broadcasted_iota(jnp.int32, (1, LANES), 1)
    causal = lax.broadcasted_iota(jnp.int32, (rows, rows), 0) >= lax.broadcasted_iota(jnp.int32, (rows, rows), 1)

    own_log[...] = jnp.zeros_like(own_log)
    for g in range(quads):
        wait(recv_sem, 0, g, spread[g])
        local[g][0].wait()

        asked[g][my_rows, :] = spread[g][source_ref[me]]

        @pl.loop(1, n)
        def _(k):
            to = lax.rem(me + k, n)
            staged[g][to] = spread[g][source_ref[to]]
            send(1, g, staged[g].at[to], asked[g].at[my_rows], to)

    for g in range(quads):
        local[g][1].wait()
        tiles, logs = attend_quad(
            lambda s, w: own[g, 0, :, s : s + w],
            lambda s, w: own[g, 1, :, s : s + w],
            lambda s, w: own[g, 2, :, s : s + w],
            causal,
        )
        for i, tile in enumerate(tiles):
            own_mix[:, g * QUAD + i * LANES : g * QUAD + (i + 1) * LANES] = tile
        for i, log in enumerate(logs):
            own_log[...] = jnp.where(lane == g * 4 + i, log, own_log[...])

    def relay(g):
        wait(recv_sem, 2, g, landed[g])
        answer[g][my_rows, :] = landed[g][slot_ref[me]]

        @pl.loop(1, n)
        def _(k):
            to = lax.rem(me + k, n)
            restaged[g][to] = landed[g][slot_ref[to]]
            send(3, g, restaged[g].at[to], answer[g].at[my_rows], to)

    live = lax.broadcasted_iota(jnp.int32, (1, tps * positions), 1) < tables_ref[tables_ref[2 * n + me]]
    old_log[...] = jnp.zeros_like(old_log)
    for g in range(quads):
        wait_rows(recv_sem, 1, g, asked[g])
        local[g][2].wait()
        arrived = kv.at[g, :, pl.ds(0, (tps - 1) * positions)]
        pltpu.make_async_copy(arrived, arrived, kv_recv.at[g]).wait()
        tiles, logs = attend_quad(
            lambda s, w: asked[g][:, s : s + w],
            lambda s, w: kv[g, 0, :, s : s + w],
            lambda s, w: kv[g, 1, :, s : s + w],
            live,
        )
        for i, tile in enumerate(tiles):
            partial[g][:, i * LANES : (i + 1) * LANES] = tile.astype(jnp.bfloat16)
        for i, log in enumerate(logs):
            old_log[...] = jnp.where(lax.rem(lane, heads) == g * 4 + i, log, old_log[...])
        if g == quads - 1:
            log = old_log[...]
            high = log.astype(jnp.bfloat16).astype(jnp.float32)
            middle = (log - high).astype(jnp.bfloat16).astype(jnp.float32)
            low = log - high - middle
            pieces = jnp.where(lane < heads, high, jnp.where(lane < 2 * heads, middle, low))
            partial[g][:, QUAD:] = pieces.astype(jnp.bfloat16)

        landed[g][me] = partial[g][my_rows, :]

        @pl.loop(1, n)
        def _(k):
            to = lax.rem(me + k, n)
            send(
                2, g, partial[g].at[pl.ds(pl.multiple_of(to * block, block), block)], landed[g].at[me], to
            )

        if g >= 2:
            relay(g - 2)

    for g in range(max(quads - 2, 0), quads):
        relay(g)

    for g in range(quads):
        wait_rows(recv_sem, 3, g, answer[g])
    pieces = answer[quads - 1][:, QUAD:].astype(jnp.float32)
    log = pieces + pltpu.roll(pieces, LANES - heads, 1) + pltpu.roll(pieces, LANES - 2 * heads, 1)
    share = 1.0 / (1.0 + jnp.exp(own_log[...] - log))
    for g in range(quads):
        parts = [share[:, g * 4 + i : g * 4 + i + 1] for i in range(4)]
        for i, (edge, left, right) in enumerate(((96, 0, 1), (64, 1, 2), (32, 2, 3))):
            portion = jnp.where(lane < edge, parts[left], parts[right])
            columns = slice(g * QUAD + i * LANES, g * QUAD + (i + 1) * LANES)
            mine = own_mix[:, columns]
            theirs = answer[g][:, i * LANES : (i + 1) * LANES].astype(jnp.float32)
            out_ref[0, :, columns] = (mine + portion * (theirs - mine)).astype(jnp.bfloat16)

    for g in range(quads):
        wait(send_sem, 0, g, spread[g])
        wait(send_sem, 1, g, staged[g])
        wait(send_sem, 2, g, landed[g])
        wait(send_sem, 3, g, restaged[g])
        sent = kv.at[g, :, pl.ds(0, (tps - 1) * positions)]
        pltpu.make_async_copy(sent, sent, kv_send.at[g]).wait()


def fused(n, tps, cache, cache_len, group, group_req, req_order):
    rows, width = group.shape[2], group.shape[3]
    positions = cache.shape[2]
    quads = width // QUAD
    block = rows // n
    widths = [QUAD] * (quads - 1) + [QUAD + LANES]

    def blocks(sizes):
        return [pltpu.VMEM((n, block, w), jnp.bfloat16) for w in sizes]

    def whole(sizes):
        return [pltpu.VMEM((rows, w), jnp.bfloat16) for w in sizes]

    plain = [QUAD] * quads
    return pl.pallas_call(
        functools.partial(kernel, n, tps, quads),
        out_shape=jax.ShapeDtypeStruct((1, rows, width), jnp.bfloat16),
        in_specs=[pl.BlockSpec(memory_space=pl.ANY)] * 3,
        out_specs=pl.BlockSpec(memory_space=pltpu.VMEM),
        scratch_shapes=[
            pltpu.SMEM((3 * n,), jnp.int32),
            *[pltpu.SMEM((n,), jnp.int32)] * 2,
            pltpu.VMEM((quads, 2, tps * positions, QUAD), jnp.bfloat16),
            pltpu.VMEM((quads, 3, rows, QUAD), jnp.bfloat16),
            pltpu.VMEM((rows, width), jnp.float32),
            pltpu.VMEM((rows, LANES), jnp.float32),
            pltpu.VMEM((rows, LANES), jnp.float32),
            *blocks(plain), *blocks(plain), *whole(plain), *whole(widths),
            *blocks(widths), *blocks(widths), *whole(widths),
            pltpu.SemaphoreType.DMA((4, quads)),
            pltpu.SemaphoreType.DMA((4, quads)),
            pltpu.SemaphoreType.DMA((quads,)),
            pltpu.SemaphoreType.DMA((quads,)),
            pltpu.SemaphoreType.DMA((3, quads)),
            pltpu.SemaphoreType.DMA((1,)),
        ],
        compiler_params=pltpu.CompilerParams(
            collective_id=0, has_side_effects=True, vmem_limit_bytes=53 * 2**20
        ),
        cost_estimate=pl.CostEstimate(
            flops=4 * rows * width * (rows + tps * positions),
            bytes_accessed=cache.size * 2 + group.size * 2,
            transcendentals=rows * (rows + tps * positions) * width // HD,
        ),
    )(jnp.concatenate((cache_len, group_req, req_order)), cache, group)


def pick(array, index):
    return jnp.stack(
        [lax.dynamic_index_in_dim(array, index[i], 1, keepdims=False) for i in range(array.shape[1])], axis=1
    )


def inverse_table(permutation):
    numbers = jnp.arange(permutation.shape[0], dtype=jnp.int32)
    matches = permutation[None, :] == numbers[:, None]
    return jnp.sum(jnp.where(matches, numbers[None, :], 0), axis=1)


def online_part(queries, key_rows, value_rows, keep_rows, block_rows, block_count, factor):
    row_count = queries.shape[0]
    head_count = queries.shape[1]

    def add_block(block_index, carry):
        row_top, weight_sum, weighted = carry
        block_start = block_index * block_rows
        scores = (
            jnp.einsum("qhd,khd->hqk", queries, key_rows, preferred_element_type=jnp.float32)
            * factor
        )
        scores = jnp.where(keep_rows(block_start)[None], scores, -jnp.inf)
        new_top = jnp.maximum(row_top, jnp.max(scores, axis=-1))
        rescale = jnp.exp(row_top - new_top)
        weights = jnp.exp(scores - new_top[..., None]).astype(jnp.bfloat16)
        weight_sum = weight_sum * rescale + jnp.sum(weights, axis=-1, dtype=jnp.float32)
        weighted = weighted * rescale[..., None] + jnp.einsum(
            "hqk,khd->hqd", weights, value_rows, preferred_element_type=jnp.float32
        )
        return (new_top, weight_sum, weighted)

    start_top = jnp.full((head_count, row_count), -jnp.inf, jnp.float32)
    start_sum = jnp.zeros((head_count, row_count), jnp.float32)
    start_mixed = jnp.zeros((head_count, row_count, queries.shape[2]), jnp.float32)
    return lax.fori_loop(0, block_count, add_block, (start_top, start_sum, start_mixed))


def combine_parts(first_part, second_part):
    top_one, sum_one, mixed_one = first_part
    top_two, sum_two, mixed_two = second_part
    row_top = jnp.maximum(top_one, top_two)
    factor_one = jnp.exp(top_one - row_top)
    factor_two = jnp.exp(top_two - row_top)
    result = (factor_one[..., None] * mixed_one + factor_two[..., None] * mixed_two) / (
        factor_one * sum_one + factor_two * sum_two
    )[..., None]
    result = jnp.transpose(result, (1, 0, 2))
    return result.reshape(result.shape[0], -1).astype(jnp.bfloat16)


def shards(cache, cache_len, group, group_req, req_order):
    factor = 1.0 / math.sqrt(HD)
    slot_of = inverse_table(req_order)
    source_slot = jnp.take(slot_of, group_req)
    my_request = jnp.take(group_req, lax.axis_index("seq"))
    length = jnp.take(cache_len, my_request)
    row_count = group.shape[2]
    head_count = group.shape[3] // HD
    queries = group[0, 0].reshape(row_count, head_count, HD)
    new_keys = group[1, 0].reshape(row_count, head_count, HD)
    new_values = group[2, 0].reshape(row_count, head_count, HD)
    group_block = min(512, row_count)

    def causal_rows(block_start):
        key_index = block_start + jnp.arange(group_block, dtype=jnp.int32)
        return jnp.arange(row_count, dtype=jnp.int32)[:, None] >= key_index[None, :]

    group_part = online_part(
        queries, new_keys, new_values, causal_rows, group_block, row_count // group_block, factor
    )
    spread = lax.all_to_all(cache, "seq", split_axis=2, concat_axis=1, tiled=True)
    ordered = pick(spread, source_slot)
    moved = lax.all_to_all(
        lax.all_to_all(ordered, "seq", split_axis=1, concat_axis=2, tiled=True),
        "tp",
        split_axis=3,
        concat_axis=2,
        tiled=True,
    )
    position_count = moved.shape[2]
    old_keys = moved[0, 0].reshape(position_count, head_count, HD)
    old_values = moved[1, 0].reshape(position_count, head_count, HD)
    cache_block = min(512, position_count)

    def live_rows(block_start):
        positions = block_start + jnp.arange(cache_block, dtype=jnp.int32)
        return (positions < length)[None, :]

    block_total = position_count // cache_block
    cache_part = online_part(
        queries, old_keys, old_values, live_rows, cache_block, block_total, factor
    )
    context = combine_parts(cache_part, group_part)
    return context[None]


def solution(mesh):
    n, tps = mesh.shape["seq"], mesh.shape["tp"]

    def run(cache, cache_len, group, group_req, req_order):
        rows, width = group.shape[2], group.shape[3]
        whole_blocks = rows % (16 * n) == 0 and width % QUAD == 0 and 3 * (width // HD) <= LANES
        if whole_blocks and tps > 1 and cache.shape[2] % 16 == 0:
            return fused(n, tps, cache, cache_len, group, group_req, req_order)
        return shards(cache, cache_len, group, group_req, req_order)

    in_specs = (P(None, "seq", "tp", None), P(), P(None, "seq", None, "tp"), P(), P())
    out_specs = P("seq", None, "tp")
    return jax.shard_map(run, mesh=mesh, in_specs=in_specs, out_specs=out_specs, check_vma=False)
```
